32 devices in a mesh: groups: 2 (over y), feat: 8 (over z, x), corp: 2 (over core).
Axes of the slice: x: 2, y: 2, z: 4, core: 2. Of those that a mesh axis runs over, the one named last changes fastest.
Arguments:
- query_features: bfloat16 [1536, 16384], P(('groups', 'corp'), 'feat'), parts along dimension 0, may hold values from -6 to 6
- inverse_kernel: bfloat16 [16384, 16384], P(None, 'feat'), may hold values from -1 to 3, as said below
- doc_features: bfloat16 [512, 16384], P(('groups', 'corp'), 'feat'), parts along dimension 0, may hold values from -0.046875 to 0.046875
Outputs:
- scores: float32 [1536, 256], P(('groups', 'feat'), 'corp'), parts along dimension 0
The draws below stay inside these ranges and needn't reach their ends.
There are 2 independent parts, one for each index of `groups`. The reference program is written for one: setup_inputs(seed, part) draws one part's arguments, and reference() takes and returns one part's arrays. A program takes and returns all parts, laid end to end along the dimension named above; an argument that names none is the same for every part. Nothing has to cross between parts.
Inputs may be any that keep to these rules, and one draw needn't show every extreme that they name: inverse_kernel is symmetric.
All inputs are finite; a program needn't handle non-finite values.
Results may differ from the reference program's by a relative error of at most 0.0003.
Values may be sent and summed in bfloat16 or wider, within the bound.
A program may use at most 128 MiB of HBM per device.

```python
import math
import jax
import jax.numpy as jnp
from jax import lax

K = 16384
QUERIES = 768
DOCS = 256


def draw_inverse_kernel(key, part):
    noise_key, diag_key = jax.random.split(key)
    noise = jnp.clip(jax.random.normal(noise_key, (K, K), jnp.float32), -4.0, 4.0)
    diag_values = 0.5 + 2.0 * jax.random.uniform(diag_key, (K,), jnp.float32)
    symmetric = (noise + noise.T) * (math.sqrt(0.5) / math.sqrt(K))
    row_index = iota_rows()
    diagonal_mask = row_index == row_index.T
    return jnp.where(diagonal_mask, diag_values[None, :], symmetric).astype(jnp.bfloat16)


def iota_rows():
    return jnp.arange(K, dtype=jnp.int32)[:, None] + jnp.zeros((1, K), jnp.int32)


def levels(key, extent, cuts, low, largest):
    def one(position, blocks):
        heights = jax.random.uniform(jax.random.fold_in(jax.random.fold_in(key, 6), position), (blocks,), jnp.float32, low / len(cuts), largest / len(cuts))
        return jnp.repeat(jnp.exp(heights), extent[position] // blocks).reshape((-1,) + (1,) * (len(extent) - position - 1))

    gain = one(*cuts[0])
    for cut in cuts[1:]:
        gain = gain * one(*cut)
    return gain


def centred(key, dims, spread, most, shards=(), kind=jnp.bfloat16):
    level = levels(key, dims, shards, -0.22, 0.18) if shards else 1.0
    array = jax.random.normal(key, dims, jnp.float32) * spread * level
    return jnp.minimum(jnp.maximum(array, -most), most).astype(kind)


def setup_inputs(seed: int = 0, part: int = 0) -> dict:
    arg_keys = jax.random.split(jax.random.key(seed), 4)
    part_keys = jax.random.split(jax.random.fold_in(arg_keys[3], part), 4)
    query_features = centred(part_keys[0], (QUERIES, K), 1.0, 6.0, ((0, 2), (1, 8)))
    inverse_kernel = draw_inverse_kernel(jax.random.fold_in(arg_keys[3], 71), part)
    doc_features = centred(part_keys[2], (DOCS, K), K ** -0.5, 0.046875, ((0, 2), (1, 8)))
    return dict(query_features=query_features, inverse_kernel=inverse_kernel, doc_features=doc_features)


def reference(query_features, inverse_kernel, doc_features):
    precond = jnp.dot(query_features, inverse_kernel, preferred_element_type=jnp.float32)
    return jnp.dot(precond, doc_features.astype(jnp.float32).T, precision=lax.Precision.HIGHEST)
```

```python
import functools

import jax
import jax.numpy as jnp
from jax import lax
from jax.experimental import pallas as pl
from jax.experimental.pallas import tpu as pltpu
from jax.sharding import PartitionSpec as P

MESH = pl.DeviceIdType.MESH
PIECES = 2
SLOTS = 8
TILE = 512


def plan(depth, pieces):
    keep = pieces // 2

    def partner(z):
        return z ^ 1 if depth % 2 == 0 else -1

    plans = []
    for z in range(depth):
        same = []
        for b in range(depth):
            for h in range(pieces):
                near = abs(b - z)
                when = 0 if near == 0 else pieces * (near - 1) + h + 1
                up = b <= z and z + 1 < depth
                down = b >= z and z > 0
                across = not (b == partner(z) and h >= keep)
                same.append((when, 1, b, h, up, down, across))
        same.sort(key=lambda e: (e[0], e[2] != partner(z), e[3]))
        other, clock = [], 0
        for when, _, b, h, _, _, across in same:
            if across:
                clock = max(clock, when) + 1
                sent = b == z and h >= keep and partner(z) >= 0
                up = sent and partner(z) > z
                down = sent and partner(z) < z
                other.append((clock + 0.5, 0, b, h, up, down, False))
        count = 0
        for b in range(depth):
            for h in range(keep, pieces):
                if b == partner(z):
                    count += 1
                    line = z + 1 if b < z else depth - z
                    if b > z:
                        line = depth - 1 - z
                    else:
                        line = z
                    other.append((pieces * line + count, 0, b, h, False, False, False))
        mine = [e for e in same if e[2] == z]
        rest = sorted([e for e in same if e[2] != z] + other, key=lambda e: e[0])
        plans.append([e[1:] for e in mine + rest])
    return plans


def kernel(
    feats, q_ref, k_ref, d_ref, out_ref,
    docs, queries, slabs, acc, split, part, got,
    slab_sem, own_sem, send_sem, recv_sem, q_sem, part_send, part_recv,
):
    depth = feats // 2
    f, c = lax.axis_index("feat"), lax.axis_index("corp")
    z, x = f // 2, f % 2
    plans = plan(depth, PIECES)
    steps = feats * PIECES
    width = docs.shape[2]
    n_docs = docs.shape[1]

    def pick(values):
        values = [int(v) for v in values]
        if len(set(values)) == 1:
            return values[0]
        result = jnp.int32(values[0])
        for at in range(1, depth):
            result = jnp.where(z == at, jnp.int32(values[at]), result)
        return result

    def event(n):
        same, b, h, up, down, across = (
            pick([plans[at][n][i] for at in range(depth)]) for i in range(6)
        )
        column = same * x + (1 - same) * (1 - x)
        return (b * 2 + column) * PIECES + h, up, down, across

    events = [event(n) for n in range(steps)]

    def slab_copy(n):
        p = events[n][0]
        return pltpu.make_async_copy(
            k_ref.at[pl.ds(pl.multiple_of(p * width, width), width), :],
            slabs.at[n % SLOTS],
            slab_sem.at[n % SLOTS],
        )

    own = [
        pltpu.make_async_copy(
            d_ref.at[:, pl.ds(h * width, width)], docs.at[f * PIECES + h], own_sem.at[h]
        )
        for h in range(PIECES)
    ]
    for copy in own:
        copy.start()
    own_q = pltpu.make_async_copy(q_ref, queries.at[c], q_sem.at[0])

    barrier = pltpu.get_barrier_semaphore()
    for away in range(1, feats):
        pl.semaphore_signal(
            barrier, inc=1, device_id={"feat": (f + away) % feats}, device_id_type=MESH
        )
    pl.semaphore_signal(barrier, inc=1, device_id={"corp": 1 - c}, device_id_type=MESH)
    for n in range(min(2, steps)):
        slab_copy(n).start()
    pl.semaphore_wait(barrier, feats)

    def piece_copy(p, way):
        to = (f + 2, f - 2, z * 2 + 1 - x)[way]
        return pltpu.make_async_remote_copy(
            src_ref=docs.at[p],
            dst_ref=docs.at[p],
            send_sem=send_sem.at[way, p],
            recv_sem=recv_sem.at[p],
            device_id={"feat": to},
            device_id_type=MESH,
        )

    def when(flag, action):
        if isinstance(flag, int):
            if flag:
                action()
        else:
            pl.when(flag == 1)(action)

    def pass_on(n):
        p, *ways = events[n]
        for way in (2, 0, 1):
            when(ways[way], lambda way=way: piece_copy(p, way).start())

    for n in range(PIECES):
        own[n].wait()
        pass_on(n)
    send_q = pltpu.make_async_remote_copy(
        src_ref=q_ref,
        dst_ref=queries.at[c],
        send_sem=q_sem.at[1],
        recv_sem=q_sem.at[2],
        device_id={"corp": 1 - c},
        device_id_type=MESH,
    )
    for n in range(min(2, steps), min(SLOTS, steps)):
        slab_copy(n).start()
    own_q.start()
    send_q.start()

    for n in range(steps):
        p = events[n][0]
        if n >= PIECES:
            piece_copy(p, 2).wait_recv()
            pass_on(n)
        slab_copy(n).wait()

        def tile(j, carry, n=n, p=p):
            columns = pl.ds(pl.multiple_of(j * TILE, TILE), TILE)
            term = jnp.dot(
                docs[p], slabs[n % SLOTS, :, columns], preferred_element_type=jnp.float32
            )
            acc[:, columns] = term if n == 0 else acc[:, columns] + term
            return carry

        lax.fori_loop(0, acc.shape[1] // TILE, tile, 0)
        if n + SLOTS < steps:
            slab_copy(n + SLOTS).start()

    high = acc[...].astype(jnp.bfloat16)
    split[:n_docs, :] = high
    split[n_docs:, :] = (acc[...] - high.astype(jnp.float32)).astype(jnp.bfloat16)
    own_q.wait()
    send_q.wait()

    rows = got.shape[1]
    halves = queries.shape[1] // rows

    def part_copy(to):
        return pltpu.make_async_remote_copy(
            src_ref=part.at[to],
            dst_ref=got.at[f],
            send_sem=part_send.at[to],
            recv_sem=part_recv.at[f],
            device_id={"feat": to},
            device_id_type=MESH,
        )

    def score(to):
        left = queries[to // halves, pl.ds(pl.multiple_of((to % halves) * rows, rows), rows), :]
        both = lax.dot_general(
            left, split[...], (((1,), (1,)), ((), ())), preferred_element_type=jnp.float32
        )
        return both[:, :n_docs] + both[:, n_docs:]

    def send_part(i, carry):
        to = (f + i) % feats
        part[to] = score(to)
        part_copy(to).start()
        return carry

    lax.fori_loop(1, feats, send_part, 0)
    got[f] = score(f)

    def take(i, carry):
        source = (f + i) % feats
        pltpu.make_async_remote_copy(
            src_ref=part.at[source],
            dst_ref=got.at[source],
            send_sem=part_send.at[source],
            recv_sem=part_recv.at[source],
            device_id={"feat": source},
            device_id_type=MESH,
        ).wait()
        return carry

    lax.fori_loop(1, feats, take, 0)
    total = got[0]
    for i in range(1, feats):
        total = total + got[i]
    out_ref[...] = total

    for n in range(steps):
        p, *ways = events[n]
        for way in range(3):
            when(ways[way], lambda way=way, p=p: piece_copy(p, way).wait_send())


def fused(feats, query_features, inverse_kernel, doc_features):
    n_docs, block = doc_features.shape
    n_queries = query_features.shape[0]
    rows = 2 * n_queries // feats
    width = block // PIECES
    return pl.pallas_call(
        functools.partial(kernel, feats),
        out_shape=jax.ShapeDtypeStruct((rows, n_docs), jnp.float32),
        in_specs=[pl.BlockSpec(memory_space=pl.ANY)] * 3,
        out_specs=pl.BlockSpec(memory_space=pltpu.VMEM),
        scratch_shapes=[
            pltpu.VMEM((feats * PIECES, n_docs, width), jnp.bfloat16),
            pltpu.VMEM((2, n_queries, block), jnp.bfloat16),
            pltpu.VMEM((SLOTS, width, block), jnp.bfloat16),
            pltpu.VMEM((n_docs, block), jnp.float32),
            pltpu.VMEM((2 * n_docs, block), jnp.bfloat16),
            pltpu.VMEM((feats, rows, n_docs), jnp.float32),
            pltpu.VMEM((feats, rows, n_docs), jnp.float32),
            pltpu.SemaphoreType.DMA((SLOTS,)),
            pltpu.SemaphoreType.DMA((PIECES,)),
            pltpu.SemaphoreType.DMA((3, feats * PIECES)),
            pltpu.SemaphoreType.DMA((feats * PIECES,)),
            pltpu.SemaphoreType.DMA((3,)),
            pltpu.SemaphoreType.DMA((feats,)),
            pltpu.SemaphoreType.DMA((feats,)),
        ],
        compiler_params=pltpu.CompilerParams(
            collective_id=0, has_side_effects=True, vmem_limit_bytes=56 * 2**20
        ),
        cost_estimate=pl.CostEstimate(
            flops=2 * n_docs * inverse_kernel.shape[0] * block,
            bytes_accessed=2 * inverse_kernel.shape[0] * block,
            transcendentals=0,
        ),
    )(query_features, inverse_kernel, doc_features)


def with_collectives(query_features, inverse_kernel, doc_features):
    applied = jnp.dot(
        lax.all_gather(doc_features, "feat", axis=1, tiled=True),
        inverse_kernel,
        preferred_element_type=jnp.float32,
    )
    left_rows = lax.all_gather(query_features, "corp", axis=0, tiled=True).astype(jnp.float32)
    return lax.psum_scatter(
        lax.dot_general(
            left_rows,
            applied,
            (((1,), (1,)), ((), ())),
            precision=lax.Precision.HIGHEST,
            preferred_element_type=jnp.float32,
        ),
        "feat",
        scatter_dimension=0,
        tiled=True,
    )


def solution(mesh):
    feats = mesh.shape["feat"]

    def on_device(query_features, inverse_kernel, doc_features):
        block, rows = doc_features.shape[1], 2 * query_features.shape[0] // feats
        fits = feats in (4, 8) and mesh.shape["corp"] == 2 and block % TILE == 0 and rows % 16 == 0
        if not fits:
            return with_collectives(query_features, inverse_kernel, doc_features)
        return fused(feats, query_features, inverse_kernel, doc_features)

    placed = (P(("groups", "corp"), "feat"), P(None, "feat"), P(("groups", "corp"), "feat"))
    return jax.shard_map(
        on_device,
        mesh=mesh,
        in_specs=placed,
        out_specs=P(("groups", "feat"), "corp"),
        check_vma=False,
    )
```

```python
import functools

import jax
import jax.numpy as jnp
from jax import lax
from jax.experimental import pallas as pl
from jax.experimental.pallas import tpu as pltpu
from jax.sharding import PartitionSpec as P

MESH = pl.DeviceIdType.MESH
PIECES = 4
SLOTS = 16
TILE = 512


def plan(depth, pieces):
    keep = pieces // 2

    def partner(z):
        return z ^ 1 if depth % 2 == 0 else -1

    plans = []
    for z in range(depth):
        same = []
        for b in range(depth):
            for h in range(pieces):
                near = abs(b - z)
                when = 0 if near == 0 else pieces * (near - 1) + h + 1
                up = b <= z and z + 1 < depth
                down = b >= z and z > 0
                across = not (b == partner(z) and h >= keep)
                same.append((when, 1, b, h, up, down, across))
        same.sort(key=lambda e: (e[0], e[2] != partner(z), e[3]))
        other, clock = [], 0
        for when, _, b, h, _, _, across in same:
            if across:
                clock = max(clock, when) + 1
                other.append((clock + 0.5, 0, b, h, False, False, False))
        count = 0
        for b in range(depth):
            for h in range(keep, pieces):
                if b == partner(z):
                    count += 1
                    other.append((2 * pieces * depth + count, 0, b, h, False, False, False))
        mine = [e for e in same if e[2] == z]
        rest = sorted([e for e in same if e[2] != z] + other, key=lambda e: e[0])
        plans.append([e[1:] for e in mine + rest])
    return plans


def kernel(
    feats, q_ref, k_ref, d_ref, out_ref,
    docs, queries, slabs, acc, split, part, got,
    slab_sem, own_sem, send_sem, recv_sem, q_sem, part_send, part_recv,
):
    depth = feats // 2
    f, c = lax.axis_index("feat"), lax.axis_index("corp")
    z, x = f // 2, f % 2
    plans = plan(depth, PIECES)
    detour = range(PIECES // 2, PIECES) if depth % 2 == 0 else range(0)
    ready = [
        max(n for n, e in enumerate(p) if e[0] == 1 or (e[1] == at and e[2] in detour))
        for at, p in enumerate(plans)
    ]
    steps = feats * PIECES
    width = docs.shape[2]
    n_docs = docs.shape[1]

    def pick(values):
        values = [int(v) for v in values]
        if len(set(values)) == 1:
            return values[0]
        result = jnp.int32(values[0])
        for at in range(1, depth):
            result = jnp.where(z == at, jnp.int32(values[at]), result)
        return result

    def event(n):
        same, b, h, up, down, across = (
            pick([plans[at][n][i] for at in range(depth)]) for i in range(6)
        )
        column = same * x + (1 - same) * (1 - x)
        return (b * 2 + column) * PIECES + h, up, down, across

    events = [event(n) for n in range(steps)]

    def slab_copy(n):
        p = events[n][0]
        return pltpu.make_async_copy(
            k_ref.at[pl.ds(pl.multiple_of(p * width, width), width), :],
            slabs.at[n % SLOTS],
            slab_sem.at[n % SLOTS],
        )

    own = [
        pltpu.make_async_copy(
            d_ref.at[:, pl.ds(h * width, width)], docs.at[f * PIECES + h], own_sem.at[h]
        )
        for h in range(PIECES)
    ]
    for copy in own:
        copy.start()
    own_q = pltpu.make_async_copy(q_ref, queries.at[c], q_sem.at[0])

    barrier = pltpu.get_barrier_semaphore()
    for away in range(1, feats):
        pl.semaphore_signal(
            barrier, inc=1, device_id={"feat": (f + away) % feats}, device_id_type=MESH
        )
    pl.semaphore_signal(barrier, inc=1, device_id={"corp": 1 - c}, device_id_type=MESH)
    for n in range(min(2, steps)):
        slab_copy(n).start()
    pl.semaphore_wait(barrier, feats)

    def piece_copy(p, way):
        to = (f + 2, f - 2, z * 2 + 1 - x, f + 2 - 4 * (z % 2))[way]
        return pltpu.make_async_remote_copy(
            src_ref=docs.at[p],
            dst_ref=docs.at[p],
            send_sem=send_sem.at[way, p],
            recv_sem=recv_sem.at[p],
            device_id={"feat": to},
            device_id_type=MESH,
        )

    def when(flag, action):
        if isinstance(flag, int):
            if flag:
                action()
        else:
            pl.when(flag == 1)(action)

    def detours():
        return [piece_copy((z * 2 + 1 - x) * PIECES + h, 3) for h in detour]

    def start_detours():
        for copy in detours():
            copy.start()

    def pass_on(n):
        p, *ways = events[n]
        for way in (2, 0, 1):
            when(ways[way], lambda way=way: piece_copy(p, way).start())
        when(pick([at == n for at in ready]), start_detours)

    for n in range(PIECES):
        own[n].wait()
        pass_on(n)
    send_q = pltpu.make_async_remote_copy(
        src_ref=q_ref,
        dst_ref=queries.at[c],
        send_sem=q_sem.at[1],
        recv_sem=q_sem.at[2],
        device_id={"corp": 1 - c},
        device_id_type=MESH,
    )
    for n in range(min(2, steps), min(SLOTS, steps)):
        slab_copy(n).start()
    own_q.start()
    send_q.start()

    for n in range(steps):
        p = events[n][0]
        if n >= PIECES:
            piece_copy(p, 2).wait_recv()
            pass_on(n)
        slab_copy(n).wait()

        def tile(j, carry, n=n, p=p):
            columns = pl.ds(pl.multiple_of(j * TILE, TILE), TILE)
            term = jnp.dot(
                docs[p], slabs[n % SLOTS, :, columns], preferred_element_type=jnp.float32
            )
            acc[:, columns] = term if n == 0 else acc[:, columns] + term
            return carry

        lax.fori_loop(0, acc.shape[1] // TILE, tile, 0)
        if n + SLOTS < steps:
            slab_copy(n + SLOTS).start()

    high = acc[...].astype(jnp.bfloat16)
    split[:n_docs, :] = high
    split[n_docs:, :] = (acc[...] - high.astype(jnp.float32)).astype(jnp.bfloat16)
    own_q.wait()
    send_q.wait()

    rows = got.shape[1]
    halves = queries.shape[1] // (2 * rows)

    def part_copy(to):
        return pltpu.make_async_remote_copy(
            src_ref=part.at[to],
            dst_ref=got.at[f],
            send_sem=part_send.at[to],
            recv_sem=part_recv.at[f],
            device_id={"feat": to},
            device_id_type=MESH,
        )

    def score(level):
        start = pl.multiple_of((level % halves) * 2 * rows, 2 * rows)
        both = lax.dot_general(
            queries[level // halves, pl.ds(start, 2 * rows), :],
            split[...],
            (((1,), (1,)), ((), ())),
            preferred_element_type=jnp.float32,
        )
        both = both[:, :n_docs] + both[:, n_docs:]
        part[level * 2] = both[:rows]
        part[level * 2 + 1] = both[rows:]

    def send_parts(i, carry):
        level = (z + i) % depth
        score(level)
        part_copy(level * 2 + x).start()
        part_copy(level * 2 + 1 - x).start()
        return carry

    lax.fori_loop(1, depth, send_parts, 0)
    score(z)
    part_copy(z * 2 + 1 - x).start()
    got[f] = part[f]

    def take(i, carry):
        source = (f + i) % feats
        pltpu.make_async_remote_copy(
            src_ref=part.at[source],
            dst_ref=got.at[source],
            send_sem=part_send.at[source],
            recv_sem=part_recv.at[source],
            device_id={"feat": source},
            device_id_type=MESH,
        ).wait()
        return carry

    lax.fori_loop(1, feats, take, 0)
    total = got[0]
    for i in range(1, feats):
        total = total + got[i]
    out_ref[...] = total

    for n in range(steps):
        p, *ways = events[n]
        for way in range(3):
            when(ways[way], lambda way=way, p=p: piece_copy(p, way).wait_send())
    for copy in detours():
        copy.wait_send()


def fused(feats, query_features, inverse_kernel, doc_features):
    n_docs, block = doc_features.shape
    n_queries = query_features.shape[0]
    rows = 2 * n_queries // feats
    width = block // PIECES
    return pl.pallas_call(
        functools.partial(kernel, feats),
        out_shape=jax.ShapeDtypeStruct((rows, n_docs), jnp.float32),
        in_specs=[pl.BlockSpec(memory_space=pl.ANY)] * 3,
        out_specs=pl.BlockSpec(memory_space=pltpu.VMEM),
        scratch_shapes=[
            pltpu.VMEM((feats * PIECES, n_docs, width), jnp.bfloat16),
            pltpu.VMEM((2, n_queries, block), jnp.bfloat16),
            pltpu.VMEM((SLOTS, width, block), jnp.bfloat16),
            pltpu.VMEM((n_docs, block), jnp.float32),
            pltpu.VMEM((2 * n_docs, block), jnp.bfloat16),
            pltpu.VMEM((feats, rows, n_docs), jnp.float32),
            pltpu.VMEM((feats, rows, n_docs), jnp.float32),
            pltpu.SemaphoreType.DMA((SLOTS,)),
            pltpu.SemaphoreType.DMA((PIECES,)),
            pltpu.SemaphoreType.DMA((4, feats * PIECES)),
            pltpu.SemaphoreType.DMA((feats * PIECES,)),
            pltpu.SemaphoreType.DMA((3,)),
            pltpu.SemaphoreType.DMA((feats,)),
            pltpu.SemaphoreType.DMA((feats,)),
        ],
        compiler_params=pltpu.CompilerParams(
            collective_id=0, has_side_effects=True, vmem_limit_bytes=56 * 2**20
        ),
        cost_estimate=pl.CostEstimate(
            flops=2 * n_docs * inverse_kernel.shape[0] * block,
            bytes_accessed=2 * inverse_kernel.shape[0] * block,
            transcendentals=0,
        ),
    )(query_features, inverse_kernel, doc_features)


def with_collectives(query_features, inverse_kernel, doc_features):
    applied = jnp.dot(
        lax.all_gather(doc_features, "feat", axis=1, tiled=True),
        inverse_kernel,
        preferred_element_type=jnp.float32,
    )
    left_rows = lax.all_gather(query_features, "corp", axis=0, tiled=True).astype(jnp.float32)
    return lax.psum_scatter(
        lax.dot_general(
            left_rows,
            applied,
            (((1,), (1,)), ((), ())),
            precision=lax.Precision.HIGHEST,
            preferred_element_type=jnp.float32,
        ),
        "feat",
        scatter_dimension=0,
        tiled=True,
    )


def solution(mesh):
    feats = mesh.shape["feat"]

    def on_device(query_features, inverse_kernel, doc_features):
        block, rows = doc_features.shape[1], 2 * query_features.shape[0] // feats
        fits = feats in (4, 8) and mesh.shape["corp"] == 2 and block % TILE == 0 and rows % 16 == 0
        if not fits:
            return with_collectives(query_features, inverse_kernel, doc_features)
        return fused(feats, query_features, inverse_kernel, doc_features)

    placed = (P(("groups", "corp"), "feat"), P(None, "feat"), P(("groups", "corp"), "feat"))
    return jax.shard_map(
        on_device,
        mesh=mesh,
        in_specs=placed,
        out_specs=P(("groups", "feat"), "corp"),
        check_vma=False,
    )
```
